128 devices in a mesh: ctx: 16 (over z_hi, x, core), tp: 8 (over y, z_lo).
Axes of the slice: x: 4, y: 4, z: 4 (z_hi: 2, z_lo: 2; z = z_hi * 2 + z_lo), core: 2. Of those that a mesh axis runs over, the one named last changes fastest.
Arguments:
- hidden_in: bfloat16 [4096, 2048], P('ctx'), may hold values from -6 to 6
- positions: int32 [4096], replicated, may hold values from 0 to 4095, as said below
- attend_gain: float32 [2048], replicated, may hold values from 0.5 to 1.5
- w_query: bfloat16 [2048, 2048], P(None, 'tp'), may hold values from -0.125 to 0.125
- w_key: bfloat16 [2048, 2048], P(None, 'tp'), may hold values from -0.125 to 0.125
- w_value: bfloat16 [2048, 2048], P(None, 'tp'), may hold values from -0.125 to 0.125
- w_output: bfloat16 [2048, 2048], P('tp'), may hold values from -1 to 1
- mixing_gain: float32 [2048], replicated, may hold values from 0.5 to 1.5
- w_gate: bfloat16 [2048, 8192], P(None, 'tp'), may hold values from -0.125 to 0.125
- w_up: bfloat16 [2048, 8192], P(None, 'tp'), may hold values from -0.125 to 0.125
- w_down: bfloat16 [8192, 2048], P('tp'), may hold values from -0.0625 to 0.0625
- out_cotangent: bfloat16 [4096, 2048], P('ctx'), may hold values from -6 to 6
Outputs:
- block_out: bfloat16 [4096, 2048], P('ctx')
- grad_hidden: bfloat16 [4096, 2048], P('ctx')
- grad_attend: float32 [2048], P('ctx')
- grad_query: float32 [2048, 2048], P('ctx', 'tp')
- grad_key: float32 [2048, 2048], P('ctx', 'tp')
- grad_value: float32 [2048, 2048], P('ctx', 'tp')
- grad_output: float32 [2048, 2048], P('tp', 'ctx')
- grad_mixing: float32 [2048], P('ctx')
- grad_gate: float32 [2048, 8192], P('ctx', 'tp')
- grad_up: float32 [2048, 8192], P('ctx', 'tp')
- grad_down: float32 [8192, 2048], P('tp', 'ctx')
The draws below stay inside these ranges and needn't reach their ends.
Inputs may be any that keep to these rules, and one draw needn't show every extreme that they name: positions holds each number of 0 to 4095 once, in runs of 128 consecutive rising values, each run starting at a multiple of 128; the order of the runs is drawn from the seed.
All inputs are finite; a program needn't handle non-finite values.
Results may differ from the reference program's by a relative error of at most 0.03.
Values may be sent and summed in bfloat16 or wider, within the bound.
A program may use at most 128 MiB of HBM per device.

```python
from functools import partial
import jax
import jax.numpy as jnp
from jax import lax

D = 2048
HEADS = 32
HD = 64
FF = 8192
BLK = 256
LEN = 4096


def draw_positions(key, part):
    key = jax.random.fold_in(key, 11)
    half_block = BLK // 2
    run_order = jax.random.permutation(key, LEN // half_block)
    offsets = jnp.arange(half_block, dtype=jnp.int32)
    placed = run_order.astype(jnp.int32)[:, None] * half_block + offsets[None, :]
    return placed.reshape(LEN).astype(jnp.int32)


def level_of(rng, shape, pieces, low, largest):
    level, own = 1.0, jax.random.fold_in(rng, 6)
    for position, blocks in pieces:
        steps = jnp.exp(jax.random.uniform(jax.random.fold_in(own, position), (blocks,), jnp.float32, low / len(pieces), largest / len(pieces)))
        level = level * jnp.repeat(steps, shape[position] // blocks).reshape([-1 if axis == position else 1 for axis in range(len(shape))])
    return level


def centred(stream_key, dims, deviation, limit, split=(), held_as=jnp.bfloat16):
    drawn = jax.random.normal(stream_key, dims, jnp.float32) * deviation
    if len(split) > 0:
        drawn = level_of(stream_key, dims, split, -0.22, 0.18) * drawn
    return jnp.clip(drawn, min=-limit, max=limit).astype(held_as)


def setup_inputs(seed: int = 0) -> dict:
    key_of = jax.random.split(jax.random.key(seed), 13)
    return {
        "hidden_in": centred(key_of[0], (LEN, D), 1.0, 6.0, ((0, 16),)),
        "positions": draw_positions(jax.random.fold_in(key_of[12], 71), 0),
        "attend_gain": jnp.clip(1.0 + 0.1 * jax.random.normal(key_of[2], (D,), jnp.float32), 0.5, 1.5),
        "w_query": centred(key_of[3], (D, D), D ** -0.5, 0.125, ((1, 8),)),
        "w_key": centred(key_of[4], (D, D), D ** -0.5, 0.125, ((1, 8),)),
        "w_value": centred(key_of[5], (D, D), D ** -0.5, 0.125, ((1, 8),)),
        "w_output": centred(key_of[6], (D, D), (max(D // 64, 1)) ** -0.5, 1.0, ((0, 8),)),
        "mixing_gain": jnp.clip(1.0 + 0.1 * jax.random.normal(key_of[7], (D,), jnp.float32), 0.5, 1.5),
        "w_gate": centred(key_of[8], (D, FF), D ** -0.5, 0.125, ((1, 8),)),
        "w_up": centred(key_of[9], (D, FF), D ** -0.5, 0.125, ((1, 8),)),
        "w_down": centred(key_of[10], (FF, D), FF ** -0.5, 0.0625, ((0, 8),)),
        "out_cotangent": centred(key_of[11], (LEN, D), 1.0, 6.0, ((0, 16),)),
    }


EPS = 1e-05
THETA = 130000.0
FLOOR = -1e+30
HIGH = lax.Precision.HIGHEST

@jax.custom_vjp
def low(v):
    return lax.optimization_barrier(v.astype(jnp.bfloat16)).astype(jnp.float32)

@jax.custom_vjp
def low_back(v):
    return v

def low_keep(v):
    return (low(v), None)

def low_pass(kept, grad):
    return (grad,)

def back_keep(v):
    return (v, None)

def back_low(kept, grad):
    return (low(grad),)
low.defvjp(low_keep, low_pass)
low_back.defvjp(back_keep, back_low)

def product_hi(left, right):
    return jnp.dot(left, right, precision=HIGH, preferred_element_type=jnp.float32)

def rope_tables(places):
    half_dim = HD // 2
    frequency = THETA ** (-(jnp.arange(half_dim, dtype=jnp.float32) * 2.0 / HD))
    angles = places.astype(jnp.float32)[:, None] * frequency[None, :]
    return (jnp.cos(angles)[:, None, :], jnp.sin(angles)[:, None, :])

def rotate(tensor, cosine_table, sine_table):
    half_dim = HD // 2
    lower_half = tensor[..., :half_dim]
    upper_half = tensor[..., half_dim:]
    return jnp.concatenate([lower_half * cosine_table - upper_half * sine_table, upper_half * cosine_table + lower_half * sine_table], axis=-1)

def normed(inputs, gain_vec):
    inverse = lax.rsqrt(lax.optimization_barrier(jnp.mean(inputs * inputs, axis=-1, keepdims=True)) + EPS)
    return inputs * inverse * gain_vec

def layer(positions, hidden, attend_gain, w_query, w_key, w_value, w_output, mixing_gain, w_gate, w_up, w_down):
    seq_len = hidden.shape[0]
    cosine_table, sine_table = rope_tables(positions)
    score_scale = HD ** (-0.5)
    allowed = positions[None, :] <= positions[:, None]
    normed_one = low(normed(hidden, attend_gain))

    def project(weight):
        return low_back(product_hi(normed_one, weight)).reshape(seq_len, HEADS, HD)
    query = low(rotate(project(w_query), cosine_table, sine_table))
    keys = low(rotate(project(w_key), cosine_table, sine_table))
    values = low(project(w_value))

    def one_head(triple):
        head_query, head_keys, head_values = triple
        scores = low_back(product_hi(head_query, head_keys.T) * score_scale)
        scores = jnp.where(allowed, scores, FLOOR)
        probs = jax.nn.softmax(scores, axis=-1)
        return product_hi(probs, head_values)
    context = lax.map(jax.checkpoint(one_head), (query.transpose(1, 0, 2), keys.transpose(1, 0, 2), values.transpose(1, 0, 2)))
    context = low(low_back(context.transpose(1, 0, 2).reshape(seq_len, HEADS * HD)))
    middle = hidden + low_back(product_hi(context, w_output))
    normed_two = low(normed(middle, mixing_gain))
    gate = low_back(product_hi(normed_two, w_gate))
    up_proj = low_back(product_hi(normed_two, w_up))
    inner = low(jax.nn.silu(gate) * up_proj)
    return middle + product_hi(inner, w_down)

def reference(hidden_in, positions, attend_gain, w_query, w_key, w_value, w_output, mixing_gain, w_gate, w_up, w_down, out_cotangent):
    inputs = (hidden_in.astype(jnp.float32), attend_gain.astype(jnp.float32), w_query.astype(jnp.float32), w_key.astype(jnp.float32), w_value.astype(jnp.float32), w_output.astype(jnp.float32), mixing_gain.astype(jnp.float32), w_gate.astype(jnp.float32), w_up.astype(jnp.float32), w_down.astype(jnp.float32))
    block_out, pullback = jax.vjp(partial(layer, positions), *inputs)
    grads = pullback(out_cotangent.astype(jnp.float32))
    return (block_out.astype(jnp.bfloat16), grads[0].astype(jnp.bfloat16), grads[1], grads[2], grads[3], grads[4], grads[5], grads[6], grads[7], grads[8], grads[9])
```

```python
import functools

import jax
import jax.numpy as jnp
from jax import lax
from jax.experimental import pallas as pl
from jax.experimental.pallas import tpu as pltpu
from jax.sharding import PartitionSpec as P

HD = 64
EPS = 1e-05
THETA = 130000.0
FLOOR = -1e30
MESH = pl.DeviceIdType.MESH
BF = jnp.bfloat16
F32 = jnp.float32
CTX, TP, XS = 16, 8, 4
VMEM_SPEC = pl.BlockSpec(memory_space=pltpu.VMEM)
SMEM_SPEC = pl.BlockSpec(memory_space=pltpu.SMEM)
ANY_SPEC = pl.BlockSpec(memory_space=pl.ANY)
GRANT = 60 * 1024 * 1024


def nt(left, right):
    return lax.dot_general(left, right, (((1,), (1,)), ((), ())), preferred_element_type=F32)


def nn(left, right):
    return jnp.dot(left, right, preferred_element_type=F32)


def tn(left, right):
    return lax.dot_general(left, right, (((0,), (0,)), ((), ())), preferred_element_type=F32)


def place():
    c, t = lax.axis_index("ctx"), lax.axis_index("tp")
    return c, t, c // 8, (c // 2) % 4, c % 2


def ctx_at(z, x, core):
    return lax.rem(z, 2) * 8 + lax.rem(x, 4) * 2 + core


def tp_peers(c, t):
    return [(c, lax.rem(t + i, TP)) for i in range(1, TP)]


def ctx_peers(c, t):
    return [(lax.rem(c + i, CTX), t) for i in range(1, CTX)]


def meet(peers):
    barrier = pltpu.get_barrier_semaphore()
    for peer in peers:
        pl.semaphore_signal(barrier, inc=1, device_id=peer, device_id_type=MESH)
    pl.semaphore_wait(barrier, len(peers))


def remote(src, dst, send, recv, peer):
    copy = pltpu.make_async_remote_copy(src, dst, send, recv, device_id=peer, device_id_type=MESH)
    copy.start()
    return copy


def wait_recv(copies):
    for copy in copies:
        copy.wait_recv()


def wait_send(copies):
    for copy in copies:
        copy.wait_send()


def swap_halves(v):
    lane = lax.broadcasted_iota(jnp.int32, v.shape, 1)
    width = v.shape[1]
    up, down = pltpu.roll(v, width - 32, 1), pltpu.roll(v, 32, 1)
    return jnp.where(lane % 64 < 32, up, down)


def project_kernel(x_ref, gain_ref, wq_ref, wk_ref, wv_ref, cos_ref, sin_ref, n1_ref, q_ref, kv_ref):
    x = x_ref[...].astype(F32)
    inverse = lax.rsqrt(jnp.mean(x * x, axis=-1, keepdims=True) + EPS)
    n1 = (x * inverse * gain_ref[...]).astype(BF)
    n1_ref[...] = n1
    cosine, sine = cos_ref[...], sin_ref[...]
    q = nn(n1, wq_ref[...])
    q_ref[...] = ((q * cosine + swap_halves(q) * sine).astype(BF).astype(F32) * 0.125).astype(BF)
    k = nn(n1, wk_ref[...])
    kv_ref[:, :256] = (k * cosine + swap_halves(k) * sine).astype(BF)
    kv_ref[:, 256:] = nn(n1, wv_ref[...]).astype(BF)


def project(x, gain, wq, wk, wv, cosine, sine):
    return pl.pallas_call(
        project_kernel,
        out_shape=(
            jax.ShapeDtypeStruct((256, 2048), BF),
            jax.ShapeDtypeStruct((256, 256), BF),
            jax.ShapeDtypeStruct((256, 512), BF),
        ),
        in_specs=[VMEM_SPEC] * 7,
        out_specs=[VMEM_SPEC] * 3,
        compiler_params=pltpu.CompilerParams(vmem_limit_bytes=GRANT),
        name="project",
    )(x, gain, wq, wk, wv, cosine, sine)


def gather_kernel(kv_ref, out_ref, local_sem, send, recv, fsend, frecv):
    c, t, z, x, core = place()
    partner = (ctx_at(z, x, 1 - core), t)
    steps = [(dz, dx) for dz in range(2) for dx in range(4)][1:]
    peers = [(ctx_at(z + dz, x + dx, core), t) for dz, dx in steps]
    own = pltpu.make_async_copy(kv_ref, out_ref.at[c], local_sem)
    own.start()
    meet(peers + [partner])
    copies = [
        remote(kv_ref, out_ref.at[c], send.at[i], recv.at[i], peer) for i, peer in enumerate(peers)
    ]
    forwards = [remote(kv_ref, out_ref.at[c], fsend.at[7], frecv.at[7], partner)]
    for i, (dz, dx) in enumerate(steps):
        copies[i].wait_recv()
        source = ctx_at(z + 2 - dz, x + 4 - dx, core)
        forwards.append(
            remote(out_ref.at[source], out_ref.at[source], fsend.at[i], frecv.at[i], partner)
        )
    own.wait()
    wait_recv(forwards)
    wait_send(copies + forwards)


def gather(kv):
    dma = pltpu.SemaphoreType.DMA
    return pl.pallas_call(
        gather_kernel,
        out_shape=jax.ShapeDtypeStruct((CTX, 256, 512), BF),
        in_specs=[VMEM_SPEC],
        out_specs=VMEM_SPEC,
        scratch_shapes=[dma, dma((7,)), dma((7,)), dma((8,)), dma((8,))],
        compiler_params=pltpu.CompilerParams(
            collective_id=0, has_side_effects=True, vmem_limit_bytes=GRANT
        ),
        name="gather",
    )(kv)


def spread_heads(source, target):
    lane_head = lax.broadcasted_iota(jnp.int32, source.shape, 1) // HD
    for h in range(4):
        target[h * 256 : (h + 1) * 256, :] = jnp.where(lane_head == h, source, 0.0).astype(BF)


def masked(scores, base_ref, qpos, b):
    row = lax.broadcasted_iota(jnp.int32, (128, 1024), 0)
    halves = [
        jnp.where(row <= qpos - base_ref[2 * b + r], scores[r * 128 : (r + 1) * 128], FLOOR)
        for r in range(2)
    ]
    return jnp.concatenate(halves, axis=0)


def attend_kernel(base_ref, q_ref, kv_ref, qpos_ref, o_ref, lse_ref, q4, top, total, acc):
    spread_heads(q_ref[...].astype(F32), q4)
    top[...] = jnp.full((1, 1024), FLOOR, F32)
    total[...] = jnp.zeros((1, 1024), F32)
    acc[...] = jnp.zeros((256, 256), F32)
    qpos = qpos_ref[...]

    def block(b, carry):
        scores = masked(nt(kv_ref[b, :, :256], q4[...]), base_ref, qpos, b)
        best = jnp.maximum(top[...], jnp.max(scores, axis=0, keepdims=True))
        alpha = jnp.exp(top[...] - best)
        p = jnp.exp(scores - best)
        total[...] = total[...] * alpha + jnp.sum(p, axis=0, keepdims=True)
        top[...] = best
        low = p.astype(BF)
        v_t = kv_ref[b, :, 256:].T
        for h in range(4):
            rows, cols = slice(h * HD, (h + 1) * HD), slice(h * 256, (h + 1) * 256)
            acc[rows, :] = acc[rows, :] * alpha[:, cols] + nn(v_t[rows, :], low[:, cols])
        return carry

    lax.fori_loop(0, CTX, block, 0)
    scale = 1.0 / total[...]
    for h in range(4):
        rows, cols = slice(h * HD, (h + 1) * HD), slice(h * 256, (h + 1) * 256)
        acc[rows, :] = acc[rows, :] * scale[:, cols]
    o_ref[...] = acc[...].T
    lse_ref[...] = top[...] + jnp.log(total[...])


def attend(base, q, kv, qpos):
    return pl.pallas_call(
        attend_kernel,
        out_shape=(
            jax.ShapeDtypeStruct((256, 256), F32),
            jax.ShapeDtypeStruct((1, 1024), F32),
        ),
        in_specs=[SMEM_SPEC] + [VMEM_SPEC] * 3,
        out_specs=[VMEM_SPEC] * 2,
        scratch_shapes=[
            pltpu.VMEM((1024, 256), BF),
            pltpu.VMEM((1, 1024), F32),
            pltpu.VMEM((1, 1024), F32),
            pltpu.VMEM((256, 256), F32),
        ],
        compiler_params=pltpu.CompilerParams(vmem_limit_bytes=GRANT),
        name="attend",
    )(base, q, kv, qpos)


def attend_back_kernel(
    base_ref, q_ref, kv_ref, qpos_ref, lse_ref, o_ref, da_ref, wo_ref, dq_ref, dkv_ref, q4, d4, acc
):
    spread_heads(q_ref[...].astype(F32), q4)
    dob = nt(da_ref[...], wo_ref[...]).astype(BF).astype(F32)
    spread_heads(dob, d4)
    weighted = (dob * o_ref[...]).T
    delta = jnp.concatenate(
        [jnp.sum(weighted[h * HD : (h + 1) * HD], axis=0, keepdims=True) for h in range(4)], axis=1
    )
    acc[...] = jnp.zeros((256, 256), F32)
    qpos, lse = qpos_ref[...], lse_ref[...]

    def block(b, carry):
        k, v = kv_ref[b, :, :256], kv_ref[b, :, 256:]
        p = jnp.exp(masked(nt(k, q4[...]), base_ref, qpos, b) - lse)
        ds = (p * (nt(v, d4[...]) - delta)).astype(BF)
        dkv_ref[b, :, :256] = nn(ds, q4[...]).astype(BF)
        dkv_ref[b, :, 256:] = nn(p.astype(BF), d4[...]).astype(BF)
        k_t = k.T
        for h in range(4):
            rows, cols = slice(h * HD, (h + 1) * HD), slice(h * 256, (h + 1) * 256)
            acc[rows, :] += nn(k_t[rows, :], ds[:, cols])
        return carry

    lax.fori_loop(0, CTX, block, 0)
    dq_ref[...] = acc[...].T * 0.125


def attend_back(base, q, kv, qpos, lse, o, da, wo):
    return pl.pallas_call(
        attend_back_kernel,
        out_shape=(
            jax.ShapeDtypeStruct((256, 256), F32),
            jax.ShapeDtypeStruct((CTX, 256, 512), BF),
        ),
        in_specs=[SMEM_SPEC] + [VMEM_SPEC] * 7,
        out_specs=[VMEM_SPEC] * 2,
        scratch_shapes=[
            pltpu.VMEM((1024, 256), BF),
            pltpu.VMEM((1024, 256), BF),
            pltpu.VMEM((256, 256), F32),
        ],
        compiler_params=pltpu.CompilerParams(vmem_limit_bytes=GRANT),
        name="attend_back",
    )(base, q, kv, qpos, lse, o, da, wo)


def scatter_tp(blocks, landing, send, recv, peers):
    return [
        remote(blocks.at[peer[1]], landing.at[i], send.at[i], recv.at[i], peer)
        for i, peer in enumerate(peers)
    ]


def gather_tp(blocks, t, send, recv, peers):
    return [
        remote(blocks.at[t], blocks.at[t], send.at[i], recv.at[i], peer)
        for i, peer in enumerate(peers)
    ]


def summed(own, landing):
    total = own.astype(F32)
    for i in range(TP - 1):
        total = total + landing[i].astype(F32)
    return total


def middle_kernel(
    ob_ref, wo_ref, x_ref, gain_ref, n2_ref, h_ref, part, landing, s1, r1, s2, r2
):
    c, t, *_ = place()
    peers = tp_peers(c, t)
    part[...] = nn(ob_ref[...], wo_ref[...]).astype(BF).reshape(8, 32, 2048)
    meet(peers)
    first = scatter_tp(part, landing, s1, r1, peers)
    wait_recv(first)
    h = x_ref[t].astype(F32) + summed(part[t], landing)
    h_ref[...] = h
    inverse = lax.rsqrt(jnp.mean(h * h, axis=-1, keepdims=True) + EPS)
    n2_ref[t] = (h * inverse * gain_ref[...]).astype(BF)
    second = gather_tp(n2_ref, t, s2, r2, peers)
    wait_recv(second)
    wait_send(first + second)


def middle(ob, wo, x, gain):
    dma = pltpu.SemaphoreType.DMA
    return pl.pallas_call(
        middle_kernel,
        out_shape=(
            jax.ShapeDtypeStruct((8, 32, 2048), BF),
            jax.ShapeDtypeStruct((32, 2048), F32),
        ),
        in_specs=[VMEM_SPEC] * 4,
        out_specs=[VMEM_SPEC] * 2,
        scratch_shapes=[
            pltpu.VMEM((8, 32, 2048), BF),
            pltpu.VMEM((7, 32, 2048), BF),
        ]
        + [dma((7,))] * 4,
        compiler_params=pltpu.CompilerParams(
            collective_id=1, has_side_effects=True, vmem_limit_bytes=GRANT
        ),
        name="middle",
    )(ob, wo, x, gain)


def norm_back_kernel(*refs, mixing):
    if mixing:
        (grad_ref, v_ref, res_ref, gain_ref, mix_ref, out_ref, gain_out, keep_ref, block_ref) = refs[:9]
        rest = refs[9:]
    else:
        (grad_ref, v_ref, res_ref, gain_ref, out_ref, gain_out) = refs[:6]
        rest = refs[6:]
    landing, gbuf, gland, gall, s1, r1, s2, r2, s3, r3, s4, r4, *rest = rest
    c, t, *_ = place()
    peers, others = tp_peers(c, t), ctx_peers(c, t)
    meet(peers + others)
    first = scatter_tp(grad_ref, landing, s1, r1, peers)
    if mixing:
        mix_land, s5, r5, s6, r6 = rest
        mixed = scatter_tp(mix_ref, mix_land, s5, r5, peers)
    v = v_ref[...] if mixing else v_ref[t].astype(F32)
    res = res_ref[t].astype(F32) if mixing else res_ref[...]
    inverse = lax.rsqrt(jnp.mean(v * v, axis=-1, keepdims=True) + EPS)
    unit = v * inverse
    wait_recv(first)
    grad = summed(grad_ref[t], landing)
    by_unit = grad * unit
    weighted = grad * gain_ref[...]
    result = res + inverse * (
        weighted - unit * jnp.mean(weighted * unit, axis=-1, keepdims=True)
    )
    if mixing:
        keep_ref[...] = result
    out_ref[t] = result.astype(BF)
    second = gather_tp(out_ref, t, s2, r2, peers)
    eight = by_unit[0:8] + by_unit[8:16] + by_unit[16:24] + by_unit[24:32]
    for j in range(CTX):
        gbuf[j] = eight[:, j * 128 : (j + 1) * 128]
    gains = [
        remote(gbuf.at[peer[0]], gland.at[i], s3.at[i], r3.at[i], peer)
        for i, peer in enumerate(others)
    ]
    if mixing:
        wait_recv(mixed)
        block_ref[t] = (v + summed(mix_ref[t], mix_land)).astype(BF)
        blocks = gather_tp(block_ref, t, s6, r6, peers)
    wait_recv(gains)
    part = gbuf[c]
    for i in range(CTX - 1):
        part = part + gland[i]
    gall[t] = part
    lasts = gather_tp(gall, t, s4, r4, peers)
    wait_recv(lasts)
    whole = gall[0]
    for i in range(1, TP):
        whole = whole + gall[i]
    gain_out[...] = jnp.sum(whole, axis=0, keepdims=True)
    wait_recv(second)
    wait_send(first + second + gains + lasts)
    if mixing:
        wait_recv(blocks)
        wait_send(mixed + blocks)


def norm_back(grad, v, res, gain, mix=None):
    mixing = mix is not None
    dma = pltpu.SemaphoreType.DMA
    rows = jax.ShapeDtypeStruct((8, 32, 2048), BF)
    outs = [rows, jax.ShapeDtypeStruct((1, 128), F32)]
    operands = [grad, v, res, gain]
    scratch = [
        pltpu.VMEM((7, 32, 2048), BF),
        pltpu.VMEM((CTX, 8, 128), F32),
        pltpu.VMEM((CTX - 1, 8, 128), F32),
        pltpu.VMEM((TP, 8, 128), F32),
    ]
    scratch += [dma((7,))] * 4 + [dma((15,))] * 2 + [dma((7,))] * 2
    if mixing:
        outs += [jax.ShapeDtypeStruct((32, 2048), F32), rows]
        operands.append(mix)
        scratch += [pltpu.VMEM((7, 32, 2048), BF)] + [dma((7,))] * 4
    return pl.pallas_call(
        functools.partial(norm_back_kernel, mixing=mixing),
        out_shape=outs,
        in_specs=[VMEM_SPEC] * len(operands),
        out_specs=[VMEM_SPEC] * len(outs),
        scratch_shapes=scratch,
        compiler_params=pltpu.CompilerParams(
            collective_id=2 if mixing else 3, has_side_effects=True, vmem_limit_bytes=GRANT
        ),
        name="norm_back_mixing" if mixing else "norm_back_attend",
    )(*operands)


def add_into(target, left, right, count):
    def one(i, carry):
        target[i] = (left(i).astype(F32) + right(i).astype(F32)).astype(target.dtype)
        return carry

    lax.fori_loop(0, count, one, 0)


def scatter_ctx_kernel(*refs, shapes, orders):
    n = len(shapes)
    ins, outs = refs[:n], refs[n : 2 * n]
    bufs = [refs[2 * n + 4 * i : 2 * n + 4 * i + 4] for i in range(n)]
    s1, r1, s2, r2, s3, r3 = refs[6 * n :]
    c, t, z, x, core = place()
    partner = (ctx_at(z, x, 1 - core), t)
    across = (ctx_at(z + 1, x, core), t)
    along = [(ctx_at(z, x + d, core), t) for d in (1, 2, 3)]
    meet([partner, across] + along)
    started, firsts = [], []
    for i in range(n):
        firsts.append(
            remote(ins[i].at[:, 1 - core], bufs[i][0], s1.at[i], r1.at[i], partner)
        )
    seconds = []
    for i in range(n):
        firsts[i].wait_recv()
        pair, half = bufs[i][0], ins[i]
        add_into(pair, lambda j: half[j, core], lambda j: pair[j], 8)
        copies = []
        if orders[i] == "x":
            for d in (1, 2, 3):
                for zz in range(2):
                    slot = (d - 1) * 2 + zz
                    copies.append(
                        remote(
                            pair.at[zz * 4 + lax.rem(x + d, 4)],
                            bufs[i][1].at[slot],
                            s2.at[i, slot],
                            r2.at[i, slot],
                            along[d - 1],
                        )
                    )
        else:
            copies.append(
                remote(
                    pair.at[pl.ds((1 - z) * 4, 4)], bufs[i][1], s2.at[i, 0], r2.at[i, 0], across
                )
            )
        seconds.append(copies)
    thirds = []
    for i in range(n):
        wait_recv(seconds[i])
        pair, land, mid, last = bufs[i]
        copies = []
        if orders[i] == "x":
            for zz in range(2):
                total = pair[zz * 4 + x].astype(F32)
                for d in range(3):
                    total = total + land[d * 2 + zz].astype(F32)
                mid[zz] = total.astype(BF)
            copies.append(remote(mid.at[1 - z], last.at[0], s3.at[i, 0], r3.at[i, 0], across))
        else:
            add_into(mid, lambda j: pair[z * 4 + j], lambda j: land[j], 4)
            for d in (1, 2, 3):
                copies.append(
                    remote(
                        mid.at[lax.rem(x + d, 4)],
                        last.at[d - 1],
                        s3.at[i, d - 1],
                        r3.at[i, d - 1],
                        along[d - 1],
                    )
                )
        thirds.append(copies)
    for i in range(n):
        wait_recv(thirds[i])
        _, _, mid, last = bufs[i]
        total = mid[z if orders[i] == "x" else x].astype(F32)
        for d in range(1 if orders[i] == "x" else 3):
            total = total + last[d].astype(F32)
        outs[i][...] = total
        started += [firsts[i]] + seconds[i] + thirds[i]
    wait_send(started)


def scatter_ctx(arrays, orders, collective_id, name):
    n = len(arrays)
    dma = pltpu.SemaphoreType.DMA
    shapes = [a.shape[1:] for a in arrays]
    scratch = []
    for (rows, columns), order in zip(shapes, orders):
        along_x = order == "x"
        scratch += [
            pltpu.VMEM((8, rows, columns), BF),
            pltpu.VMEM((6 if along_x else 4, rows, columns), BF),
            pltpu.VMEM((2 if along_x else 4, rows, columns), BF),
            pltpu.VMEM((1 if along_x else 3, rows, columns), BF),
        ]
    scratch += [dma((n,))] * 2 + [dma((n, 6))] * 2 + [dma((n, 3))] * 2
    return pl.pallas_call(
        functools.partial(scatter_ctx_kernel, shapes=shapes, orders=orders),
        out_shape=[jax.ShapeDtypeStruct(s, F32) for s in shapes],
        in_specs=[VMEM_SPEC] * n,
        out_specs=[VMEM_SPEC] * n,
        scratch_shapes=scratch,
        compiler_params=pltpu.CompilerParams(
            collective_id=collective_id, has_side_effects=True, vmem_limit_bytes=GRANT
        ),
        name=name,
    )(*[a.reshape(8, 2, *a.shape[1:]) for a in arrays])


def rope_tables(places):
    half_dim = HD // 2
    frequency = THETA ** (-(jnp.arange(half_dim, dtype=F32) * 2.0 / HD))
    angles = places.astype(F32)[:, None] * frequency[None, :]
    cosine, sine = jnp.cos(angles), jnp.sin(angles)
    return (
        jnp.tile(jnp.concatenate([cosine, cosine], axis=1), (1, 4)),
        jnp.tile(jnp.concatenate([-sine, sine], axis=1), (1, 4)),
    )


def swap_plain(v):
    halves = v.reshape(v.shape[0], 4, 2, 32)
    return halves[:, :, ::-1].reshape(v.shape)


def shards(
    hidden_in,
    positions,
    attend_gain,
    w_query,
    w_key,
    w_value,
    w_output,
    mixing_gain,
    w_gate,
    w_up,
    w_down,
    out_cotangent,
):
    ctx_rank = lax.axis_index("ctx")
    own_places = lax.dynamic_slice_in_dim(positions, ctx_rank * 256, 256)
    cosine, sine = rope_tables(own_places)
    base = positions.reshape(32, 128)[:, 0]
    qpos = jnp.tile(own_places, 4)[None, :]
    gain_one, gain_two = attend_gain[None, :], mixing_gain[None, :]
    tokens = lambda a: a.reshape(8, 32, 2048)

    n1, q, kv_own = project(hidden_in, gain_one, w_query, w_key, w_value, cosine, sine)
    kv = gather(kv_own)
    o, lse = attend(base, q, kv, qpos)
    ob = o.astype(BF)
    n2, h = middle(ob, w_output, tokens(hidden_in), gain_two)
    n2 = n2.reshape(256, 2048)

    gate, up = nn(n2, w_gate), nn(n2, w_up)
    sigmoid = jax.nn.sigmoid(gate)
    activated = gate * sigmoid
    inner = (activated * up).astype(BF)
    mixed = nn(inner, w_down).astype(BF)
    dz = nt(out_cotangent, w_down)
    dgate = (dz * up * sigmoid * (1.0 + gate * (1.0 - sigmoid))).astype(BF)
    dup = (dz * activated).astype(BF)
    dn2 = (nt(dgate, w_gate) + nt(dup, w_up)).astype(BF)
    da, grad_mixing, dh, block_out = norm_back(
        tokens(dn2), h, tokens(out_cotangent), gain_two, tokens(mixed)
    )
    da = da.reshape(256, 2048)

    dq, dkv = attend_back(base, q, kv, qpos, lse, o, da, w_output)
    (own_dkv,) = scatter_ctx([dkv], ["x"], 4, "scatter_keys")
    turn_back = lambda d: (d * cosine - swap_plain(d) * sine).astype(BF)
    dqraw = turn_back(dq)
    dkraw = turn_back(own_dkv[:, :256])
    dvraw = own_dkv[:, 256:].astype(BF)
    dn1 = (nt(dqraw, w_query) + nt(dkraw, w_key) + nt(dvraw, w_value)).astype(BF)
    grad_hidden, grad_attend = norm_back(tokens(dn1), tokens(hidden_in), dh, gain_one)

    weight = lambda a, b: tn(a, b).astype(BF).reshape(16, 128, -1)
    (grad_gate, grad_down, grad_up, grad_value, grad_output, grad_query, grad_key) = scatter_ctx(
        [
            weight(n2, dgate),
            weight(out_cotangent, inner),
            weight(n2, dup),
            weight(n1, dvraw),
            weight(da, ob),
            weight(n1, dqraw),
            weight(n1, dkraw),
        ],
        ["x", "z", "z", "x", "z", "x", "z"],
        5,
        "scatter_weights",
    )
    return (
        block_out.reshape(256, 2048),
        grad_hidden.reshape(256, 2048),
        grad_attend.reshape(128),
        grad_query,
        grad_key,
        grad_value,
        grad_output.T,
        grad_mixing.reshape(128),
        grad_gate,
        grad_up,
        grad_down.T,
    )


def solution(mesh):
    placed = (
        P("ctx", None),
        P(),
        P(),
        P(None, "tp"),
        P(None, "tp"),
        P(None, "tp"),
        P("tp", None),
        P(),
        P(None, "tp"),
        P(None, "tp"),
        P("tp", None),
        P("ctx", None),
    )
    return jax.shard_map(
        shards,
        mesh=mesh,
        in_specs=placed,
        out_specs=(
            P("ctx", None),
            P("ctx", None),
            P("ctx"),
            P("ctx", "tp"),
            P("ctx", "tp"),
            P("ctx", "tp"),
            P("tp", "ctx"),
            P("ctx"),
            P("ctx", "tp"),
            P("ctx", "tp"),
            P("tp", "ctx"),
        ),
        check_vma=False,
    )
```

```python
import functools

import jax
import jax.numpy as jnp
from jax import lax
from jax.experimental import pallas as pl
from jax.experimental.pallas import tpu as pltpu
from jax.sharding import PartitionSpec as P

HD = 64
EPS = 1e-05
THETA = 130000.0
FLOOR = -1e30
MESH = pl.DeviceIdType.MESH
BF = jnp.bfloat16
F32 = jnp.float32
CTX, TP, XS = 16, 8, 4
VMEM_SPEC = pl.BlockSpec(memory_space=pltpu.VMEM)
SMEM_SPEC = pl.BlockSpec(memory_space=pltpu.SMEM)
ANY_SPEC = pl.BlockSpec(memory_space=pl.ANY)
GRANT = 62 * 1024 * 1024


def nt(left, right):
    return lax.dot_general(left, right, (((1,), (1,)), ((), ())), preferred_element_type=F32)


def nn(left, right):
    return jnp.dot(left, right, preferred_element_type=F32)


def tn(left, right):
    return lax.dot_general(left, right, (((0,), (0,)), ((), ())), preferred_element_type=F32)


def place():
    c, t = lax.axis_index("ctx"), lax.axis_index("tp")
    return c, t, c // 8, (c // 2) % 4, c % 2


def ctx_at(z, x, core):
    return lax.rem(z, 2) * 8 + lax.rem(x, 4) * 2 + core


def tp_peers(c, t):
    return [(c, lax.rem(t + i, TP)) for i in range(1, TP)]


def ctx_peers(c, t):
    return [(lax.rem(c + i, CTX), t) for i in range(1, CTX)]


def meet(peers):
    barrier = pltpu.get_barrier_semaphore()
    for peer in peers:
        pl.semaphore_signal(barrier, inc=1, device_id=peer, device_id_type=MESH)
    pl.semaphore_wait(barrier, len(peers))


def remote(src, dst, send, recv, peer):
    copy = pltpu.make_async_remote_copy(src, dst, send, recv, device_id=peer, device_id_type=MESH)
    copy.start()
    return copy


def wait_recv(copies):
    for copy in copies:
        copy.wait_recv()


def wait_send(copies):
    for copy in copies:
        copy.wait_send()


def swap_halves(v):
    lane = lax.broadcasted_iota(jnp.int32, v.shape, 1)
    width = v.shape[1]
    up, down = pltpu.roll(v, width - 32, 1), pltpu.roll(v, 32, 1)
    return jnp.where(lane % 64 < 32, up, down)


def project_kernel(x_ref, gain_ref, wq_ref, wk_ref, wv_ref, cos_ref, sin_ref, n1_ref, q_ref, kv_ref):
    x = x_ref[...].astype(F32)
    inverse = lax.rsqrt(jnp.mean(x * x, axis=-1, keepdims=True) + EPS)
    n1 = (x * inverse * gain_ref[...]).astype(BF)
    n1_ref[...] = n1
    cosine, sine = cos_ref[...], sin_ref[...]
    q = nn(n1, wq_ref[...])
    q_ref[...] = ((q * cosine + swap_halves(q) * sine).astype(BF).astype(F32) * 0.125).astype(BF)
    k = nn(n1, wk_ref[...])
    kv_ref[:, :256] = (k * cosine + swap_halves(k) * sine).astype(BF)
    kv_ref[:, 256:] = nn(n1, wv_ref[...]).astype(BF)


def project(x, gain, wq, wk, wv, cosine, sine):
    return pl.pallas_call(
        project_kernel,
        out_shape=(
            jax.ShapeDtypeStruct((256, 2048), BF),
            jax.ShapeDtypeStruct((256, 256), BF),
            jax.ShapeDtypeStruct((256, 512), BF),
        ),
        in_specs=[VMEM_SPEC] * 7,
        out_specs=[VMEM_SPEC] * 3,
        compiler_params=pltpu.CompilerParams(vmem_limit_bytes=GRANT),
        name="project",
    )(x, gain, wq, wk, wv, cosine, sine)


def gather_kernel(kv_ref, out_ref, local_sem, send, recv, fsend, frecv):
    c, t, z, x, core = place()
    partner = (ctx_at(z, x, 1 - core), t)
    steps = [(dz, dx) for dz in range(2) for dx in range(4)][1:]
    peers = [(ctx_at(z + dz, x + dx, core), t) for dz, dx in steps]
    own = pltpu.make_async_copy(kv_ref, out_ref.at[c], local_sem)
    own.start()
    meet(peers + [partner])
    copies = [
        remote(kv_ref, out_ref.at[c], send.at[i], recv.at[i], peer) for i, peer in enumerate(peers)
    ]
    forwards = [remote(kv_ref, out_ref.at[c], fsend.at[7], frecv.at[7], partner)]
    for i, (dz, dx) in enumerate(steps):
        copies[i].wait_recv()
        source = ctx_at(z + 2 - dz, x + 4 - dx, core)
        forwards.append(
            remote(out_ref.at[source], out_ref.at[source], fsend.at[i], frecv.at[i], partner)
        )
    own.wait()
    wait_recv(forwards)
    wait_send(copies + forwards)


def gather(kv):
    dma = pltpu.SemaphoreType.DMA
    return pl.pallas_call(
        gather_kernel,
        out_shape=jax.ShapeDtypeStruct((CTX, 256, 512), BF),
        in_specs=[VMEM_SPEC],
        out_specs=VMEM_SPEC,
        scratch_shapes=[dma, dma((7,)), dma((7,)), dma((8,)), dma((8,))],
        compiler_params=pltpu.CompilerParams(
            collective_id=0, has_side_effects=True, vmem_limit_bytes=GRANT
        ),
        name="gather",
    )(kv)


def spread_heads(source, target):
    lane_head = lax.broadcasted_iota(jnp.int32, source.shape, 1) // HD
    for h in range(4):
        target[h * 256 : (h + 1) * 256, :] = jnp.where(lane_head == h, source, 0.0).astype(BF)


def masked(scores, base_ref, qpos, b):
    row = lax.broadcasted_iota(jnp.int32, (128, 1024), 0)
    halves = [
        jnp.where(row <= qpos - base_ref[2 * b + r], scores[r * 128 : (r + 1) * 128], FLOOR)
        for r in range(2)
    ]
    return jnp.concatenate(halves, axis=0)


def attend_kernel(base_ref, q_ref, kv_ref, qpos_ref, o_ref, lse_ref, q4, top, total, acc):
    spread_heads(q_ref[...].astype(F32), q4)
    top[...] = jnp.full((1, 1024), FLOOR, F32)
    total[...] = jnp.zeros((1, 1024), F32)
    acc[...] = jnp.zeros((256, 256), F32)
    qpos = qpos_ref[...]

    def block(b, carry):
        scores = masked(nt(kv_ref[b, :, :256], q4[...]), base_ref, qpos, b)
        best = jnp.maximum(top[...], jnp.max(scores, axis=0, keepdims=True))
        alpha = jnp.exp(top[...] - best)
        p = jnp.exp(scores - best)
        total[...] = total[...] * alpha + jnp.sum(p, axis=0, keepdims=True)
        top[...] = best
        low = p.astype(BF)
        v_t = kv_ref[b, :, 256:].T
        for h in range(4):
            rows, cols = slice(h * HD, (h + 1) * HD), slice(h * 256, (h + 1) * 256)
            acc[rows, :] = acc[rows, :] * alpha[:, cols] + nn(v_t[rows, :], low[:, cols])
        return carry

    lax.fori_loop(0, CTX, block, 0)
    scale = 1.0 / total[...]
    for h in range(4):
        rows, cols = slice(h * HD, (h + 1) * HD), slice(h * 256, (h + 1) * 256)
        acc[rows, :] = acc[rows, :] * scale[:, cols]
    o_ref[...] = acc[...].T
    lse_ref[...] = top[...] + jnp.log(total[...])


def attend(base, q, kv, qpos):
    return pl.pallas_call(
        attend_kernel,
        out_shape=(
            jax.ShapeDtypeStruct((256, 256), F32),
            jax.ShapeDtypeStruct((1, 1024), F32),
        ),
        in_specs=[SMEM_SPEC] + [VMEM_SPEC] * 3,
        out_specs=[VMEM_SPEC] * 2,
        scratch_shapes=[
            pltpu.VMEM((1024, 256), BF),
            pltpu.VMEM((1, 1024), F32),
            pltpu.VMEM((1, 1024), F32),
            pltpu.VMEM((256, 256), F32),
        ],
        compiler_params=pltpu.CompilerParams(vmem_limit_bytes=GRANT),
        name="attend",
    )(base, q, kv, qpos)


def scatter_tp(blocks, landing, send, recv, peers):
    return [
        remote(blocks.at[peer[1]], landing.at[i], send.at[i], recv.at[i], peer)
        for i, peer in enumerate(peers)
    ]


def gather_tp(blocks, t, send, recv, peers):
    return [
        remote(blocks.at[t], blocks.at[t], send.at[i], recv.at[i], peer)
        for i, peer in enumerate(peers)
    ]


def summed(own, landing):
    total = own.astype(F32)
    for i in range(TP - 1):
        total = total + landing[i].astype(F32)
    return total


def middle_kernel(
    ob_ref, wo_ref, x_ref, gain_ref, n2_ref, h_ref, part, landing, s1, r1, s2, r2
):
    c, t, *_ = place()
    peers = tp_peers(c, t)
    part[...] = nn(ob_ref[...], wo_ref[...]).astype(BF).reshape(8, 32, 2048)
    meet(peers)
    first = scatter_tp(part, landing, s1, r1, peers)
    wait_recv(first)
    h = x_ref[t].astype(F32) + summed(part[t], landing)
    h_ref[...] = h
    inverse = lax.rsqrt(jnp.mean(h * h, axis=-1, keepdims=True) + EPS)
    n2_ref[t] = (h * inverse * gain_ref[...]).astype(BF)
    second = gather_tp(n2_ref, t, s2, r2, peers)
    wait_recv(second)
    wait_send(first + second)


def middle(ob, wo, x, gain):
    dma = pltpu.SemaphoreType.DMA
    return pl.pallas_call(
        middle_kernel,
        out_shape=(
            jax.ShapeDtypeStruct((8, 32, 2048), BF),
            jax.ShapeDtypeStruct((32, 2048), F32),
        ),
        in_specs=[VMEM_SPEC] * 4,
        out_specs=[VMEM_SPEC] * 2,
        scratch_shapes=[
            pltpu.VMEM((8, 32, 2048), BF),
            pltpu.VMEM((7, 32, 2048), BF),
        ]
        + [dma((7,))] * 4,
        compiler_params=pltpu.CompilerParams(
            collective_id=1, has_side_effects=True, vmem_limit_bytes=GRANT
        ),
        name="middle",
    )(ob, wo, x, gain)


class Sems:
    def __init__(self, ref):
        self.ref, self.used = ref, 0

    def take(self, count):
        first = self.used
        self.used += count
        return lambda i=0: self.ref.at[first + i]


class Spread:
    def __init__(self, order, send, pair, land, mid, last, sems, where, peers):
        self.order, self.send, self.pair, self.land, self.mid, self.last = (
            order, send, pair, land, mid, last,
        )
        self.x, self.z = where
        self.partner, self.across, self.along = peers
        self.sems = [sems.take(n) for n in (1, 1, 6, 6, 3, 3)]

    def make(self, src, dst, phase, i, peer):
        send, recv = self.sems[2 * phase], self.sems[2 * phase + 1]
        return pltpu.make_async_remote_copy(
            src, dst, send(i), recv(i), device_id=peer, device_id_type=MESH
        )

    def first(self):
        return [self.make(self.send, self.pair, 0, 0, self.partner)]

    def second(self):
        if self.order == "z":
            source = self.pair.at[pl.ds((1 - self.z) * 4, 4)]
            return [self.make(source, self.land, 1, 0, self.across)]
        copies = []
        for d in (1, 2, 3):
            for zz in range(2):
                slot = (d - 1) * 2 + zz
                source = self.pair.at[zz * 4 + lax.rem(self.x + d, 4)]
                copies.append(
                    self.make(source, self.land.at[slot], 1, slot, self.along[d - 1])
                )
        return copies

    def third(self):
        if self.order == "x":
            return [self.make(self.mid.at[1 - self.z], self.last.at[0], 2, 0, self.across)]
        return [
            self.make(
                self.mid.at[lax.rem(self.x + d, 4)], self.last.at[d - 1], 2, d - 1, self.along[d - 1]
            )
            for d in (1, 2, 3)
        ]

    def middle(self):
        wait_recv(self.second())
        if self.order == "x":
            for zz in range(2):
                total = self.pair[zz * 4 + self.x].astype(F32)
                for d in range(3):
                    total = total + self.land[d * 2 + zz].astype(F32)
                self.mid[zz] = total.astype(BF)
        else:

            def one(j, carry):
                total = self.pair[self.z * 4 + j].astype(F32) + self.land[j].astype(F32)
                self.mid[j] = total.astype(BF)
                return carry

            lax.fori_loop(0, 4, one, 0)
        begin(self.third())

    def finish(self):
        wait_recv(self.third())
        total = self.mid[self.z if self.order == "x" else self.x].astype(F32)
        for d in range(1 if self.order == "x" else 3):
            total = total + self.last[d].astype(F32)
        return total

    def close(self):
        wait_send(self.first() + self.second() + self.third())


def spread_scratch(order, rows, columns, with_send=True):
    counts = (8, 8, 6, 2, 1) if order == "x" else (8, 8, 4, 4, 3)
    return [pltpu.VMEM((n, rows, columns), BF) for n in counts[0 if with_send else 1 :]]


def begin(copies):
    for copy in copies:
        copy.start()


def transposed(source, target):
    def one(j, carry):
        for core in range(2):
            cols = pl.ds(pl.multiple_of((2 * j + core) * 128, 128), 128)
            target[core, pl.ds(pl.multiple_of(j * 128, 128), 128), :] = source[:, cols].T
        return carry

    lax.fori_loop(0, 8, one, 0)


def outer(a_t, half, right, width, store):
    def one(j, carry):
        left = a_t[half, pl.ds(pl.multiple_of(j * 256, 256), 256), :]
        for n in range(right.shape[1] // width):
            product = nn(left, right[:, n * width : (n + 1) * width])
            rows = slice(n * 128, (n + 1) * 128)
            store(2 * j, rows, product[:128])
            store(2 * j + 1, rows, product[128:])
        return carry

    lax.fori_loop(0, 4, one, 0)


def send_half(spread, a_t, half, right, width):
    def store(block, rows, value):
        spread.send[block, rows, :] = value.astype(BF)

    outer(a_t, half, right, width, store)
    begin(spread.first())


def merge_half(spread, a_t, half, right, width):
    wait_recv(spread.first())

    def store(block, rows, value):
        total = value + spread.pair[block, rows, :].astype(F32)
        spread.pair[block, rows, :] = total.astype(BF)

    outer(a_t, half, right, width, store)
    begin(spread.second())


BIG = (("x", 0), ("z", 1), ("z", 2))
SMALL = ("x", "z", "x", "z")
N_SEMS = 400


def back_kernel(*refs):
    (
        base_ref, dn2_ref, mix_ref, h_ref, dy_ref, gain2_ref, n2_ref, dgate_ref, dup_ref, inner_ref,
        q_ref, qpos_ref, lse_ref, o_ref, ob_ref, wo_ref, cos_ref, sin_ref, gain1_ref,
        kv_hbm, wq_hbm, wk_hbm, wv_hbm, n1_hbm, x_hbm,
        block_ref, hidden_ref, gmix_ref, gattn_ref,
        fgate, fdown, fup, fo, fq, fk, fv,
        kv, wq, wk, wv, n1, x_own, dn2_own, mix_own, dh,
        land2, landm, land1, part1, da,
        gbuf, gland, gall, gbuf1, gland1, gall1,
        a_t, b_t, q4, d4, acc,
        *rest,
    ) = refs
    sems = Sems(rest.pop())
    c, t, z, x, core = place()
    peers, others = tp_peers(c, t), ctx_peers(c, t)
    partner = (ctx_at(z, x, 1 - core), t)
    across = (ctx_at(z + 1, x, core), t)
    along = [(ctx_at(z, x + d, core), t) for d in (1, 2, 3)]

    def take(n):
        got = rest[:n]
        del rest[:n]
        return got

    def spread(order, buffers):
        return Spread(order, *buffers, sems, (x, z), (partner, across, along))

    gate = spread("x", take(5))
    down = spread("z", take(5))
    up = spread("z", take(5))
    so, sq, sk, sv = [spread(order, take(5)) for order in SMALL]
    pairs, kland, kmid, klast, vland, vmid, vlast = take(7)
    keys_out = gate.send

    def tp_scatter(blocks, landing):
        send, recv = sems.take(7), sems.take(7)
        return lambda: [
            pltpu.make_async_remote_copy(
                blocks.at[p[1]], landing.at[i], send(i), recv(i), device_id=p, device_id_type=MESH
            )
            for i, p in enumerate(peers)
        ]

    def tp_gather(blocks):
        send, recv = sems.take(7), sems.take(7)
        return lambda: [
            pltpu.make_async_remote_copy(
                blocks.at[t], blocks.at[t], send(i), recv(i), device_id=p, device_id_type=MESH
            )
            for i, p in enumerate(peers)
        ]

    def gain_scatter(blocks, landing):
        send, recv = sems.take(15), sems.take(15)
        return lambda: [
            pltpu.make_async_remote_copy(
                blocks.at[p[0]], landing.at[i], send(i), recv(i), device_id=p, device_id_type=MESH
            )
            for i, p in enumerate(others)
        ]

    scatter2, scatterm, scatter1 = (
        tp_scatter(dn2_ref, land2), tp_scatter(mix_ref, landm), tp_scatter(part1, land1),
    )
    gather_da, gather_block, gather_hidden = (
        tp_gather(da), tp_gather(block_ref), tp_gather(hidden_ref),
    )
    gain2_scatter, gain2_gather = gain_scatter(gbuf, gland), tp_gather(gall)
    gain1_scatter, gain1_gather = gain_scatter(gbuf1, gland1), tp_gather(gall1)

    barrier = pltpu.get_barrier_semaphore()
    for peer in peers + others:
        pl.semaphore_signal(barrier, inc=1, device_id=peer, device_id_type=MESH)
    own_rows = pl.ds(pl.multiple_of(t * 32, 32), 32)
    local = sems.take(9)
    loads = [
        pltpu.make_async_copy(source, target, local(i))
        for i, (source, target) in enumerate(
            [
                (dn2_ref.at[t], dn2_own), (mix_ref.at[t], mix_own), (x_hbm.at[own_rows], x_own),
                (kv_hbm, kv), (wq_hbm, wq), (wk_hbm, wk), (wv_hbm, wv), (n1_hbm, n1),
            ]
        )
    ]
    begin(loads)
    transposed(n2_ref, a_t)
    transposed(dy_ref, b_t)
    pl.semaphore_wait(barrier, len(peers) + len(others))

    begin(scatter2())
    send_half(gate, a_t, 1 - core, dgate_ref, 512)
    send_half(down, b_t, 1 - core, inner_ref, 512)
    send_half(up, a_t, 1 - core, dup_ref, 512)
    for load in loads:
        load.wait()
    merge_half(gate, a_t, core, dgate_ref, 512)

    def through_norm(v, res, own, landing, gain):
        inverse = lax.rsqrt(jnp.mean(v * v, axis=-1, keepdims=True) + EPS)
        unit = v * inverse
        grad = summed(own, landing)
        by_unit = grad * unit
        weighted = grad * gain
        result = res + inverse * (
            weighted - unit * jnp.mean(weighted * unit, axis=-1, keepdims=True)
        )
        return result, by_unit[0:8] + by_unit[8:16] + by_unit[16:24] + by_unit[24:32]

    def gain_start(eight, buffer, scatter):
        for j in range(CTX):
            buffer[j] = eight[:, j * 128 : (j + 1) * 128]
        begin(scatter())

    def gain_middle(buffer, landing, everyone, scatter, gather_on):
        wait_recv(scatter())
        part = buffer[c]
        for i in range(CTX - 1):
            part = part + landing[i]
        everyone[t] = part
        begin(gather_on())

    def gain_end(everyone, gather_on, target):
        wait_recv(gather_on())
        whole = everyone[0]
        for i in range(1, TP):
            whole = whole + everyone[i]
        target[...] = jnp.sum(whole, axis=0, keepdims=True)

    wait_recv(scatter2())
    result, eight = through_norm(
        h_ref[...], dy_ref[own_rows, :].astype(F32), dn2_own[...], land2, gain2_ref[...]
    )
    dh[...] = result
    da[t] = result.astype(BF)
    begin(gather_da())
    gain_start(eight, gbuf, gain2_scatter)
    begin(scatterm())
    merge_half(down, b_t, core, inner_ref, 512)
    merge_half(up, a_t, core, dup_ref, 512)
    transposed(n1, b_t)
    spread_heads(q_ref[...].astype(F32), q4)
    acc[...] = jnp.zeros((256, 256), F32)
    wait_recv(gather_da())

    dob = nt(da[...].reshape(256, 2048), wo_ref[...]).astype(BF).astype(F32)
    spread_heads(dob, d4)
    weighted = (dob * o_ref[...]).T
    delta = jnp.concatenate(
        [jnp.sum(weighted[h * HD : (h + 1) * HD], axis=0, keepdims=True) for h in range(4)], axis=1
    )
    qpos, lse = qpos_ref[...], lse_ref[...]

    def key_block(b):
        k, v = kv[b, :, :256], kv[b, :, 256:]
        p = jnp.exp(masked(nt(k, q4[...]), base_ref, qpos, b) - lse)
        ds = (p * (nt(v, d4[...]) - delta)).astype(BF)
        k_t = k.T
        for h in range(4):
            rows, cols = slice(h * HD, (h + 1) * HD), slice(h * 256, (h + 1) * 256)
            acc[rows, :] += nn(k_t[rows, :], ds[:, cols])
        return nn(ds, q4[...]), nn(p.astype(BF), d4[...])

    def turn(i):
        return lax.rem(z + 1 + i // 4, 2), lax.rem(x + 1 + i, 4)

    wait_send(gate.first())
    psend, precv = sems.take(8), sems.take(8)

    def pair_copy(j):
        return pltpu.make_async_remote_copy(
            keys_out.at[j], pairs.at[j], psend(j), precv(j), device_id=partner, device_id_type=MESH
        )

    ksend, krecv = sems.take(6), sems.take(6)
    vsend, vrecv = sems.take(4), sems.take(4)

    def key_copy(j, slot, peer):
        return pltpu.make_async_remote_copy(
            pairs.at[j, :, pl.ds(0, 256)], kland.at[slot], ksend(slot), krecv(slot),
            device_id=peer, device_id_type=MESH,
        )

    def value_copy(j, slot):
        return pltpu.make_async_remote_copy(
            pairs.at[j, :, pl.ds(256, 256)], vland.at[slot], vsend(slot), vrecv(slot),
            device_id=across, device_id_type=MESH,
        )

    def other_core(i, carry):
        zz, xx = turn(i)
        j = zz * 4 + xx
        dk, dv = key_block(2 * j + 1 - core)
        keys_out[j, :, :256] = dk.astype(BF)
        keys_out[j, :, 256:] = dv.astype(BF)
        pair_copy(j).start()

        @pl.when(i == 4)
        def _():
            wait_recv(scatterm())
            block_ref[t] = (h_ref[...] + summed(mix_own[...], landm)).astype(BF)
            begin(gather_block())

        @pl.when(i == 6)
        def _():
            gain_middle(gbuf, gland, gall, gain2_scatter, gain2_gather)

        return carry

    lax.fori_loop(0, 8, other_core, 0)

    def this_core(i, carry):
        zz, xx = turn(i)
        j = zz * 4 + xx
        dk, dv = key_block(2 * j + core)
        pair_copy(j).wait_recv()
        pairs[j, :, :256] = (dk + pairs[j, :, :256].astype(F32)).astype(BF)
        pairs[j, :, 256:] = (dv + pairs[j, :, 256:].astype(F32)).astype(BF)

        @pl.when(xx != x)
        def _():
            d = lax.rem(xx - x + 4, 4)
            key_copy(j, (d - 1) * 2 + zz, (ctx_at(z, xx, core), t)).start()

        @pl.when(zz != z)
        def _():
            value_copy(j, xx).start()

        @pl.when(i == 1)
        def _():
            gate.middle()

        @pl.when(i == 5)
        def _():
            down.middle()

        return carry

    lax.fori_loop(0, 8, this_core, 0)

    def turn_back(d):
        return (d * cos_ref[...] - swap_halves(d) * sin_ref[...]).astype(BF)

    dqraw = turn_back(acc[...].T * 0.125)
    send_half(sq, b_t, 1 - core, dqraw, 256)
    transposed(da.reshape(256, 2048), a_t)
    send_half(so, a_t, 1 - core, ob_ref, 256)

    key_copies = [
        key_copy(zz * 4 + lax.rem(x + d, 4), (d - 1) * 2 + zz, along[d - 1])
        for d in (1, 2, 3)
        for zz in range(2)
    ]
    value_copies = [value_copy((1 - z) * 4 + xx, xx) for xx in range(4)]
    k3, v3 = sems.take(2), sems.take(6)
    key_last = pltpu.make_async_remote_copy(
        kmid.at[1 - z], klast, k3(0), k3(1), device_id=across, device_id_type=MESH
    )
    value_last = [
        pltpu.make_async_remote_copy(
            vmid.at[lax.rem(x + d, 4)], vlast.at[d - 1], v3(d - 1), v3(d + 2),
            device_id=along[d - 1], device_id_type=MESH,
        )
        for d in (1, 2, 3)
    ]
    wait_recv(value_copies)
    for xx in range(4):
        vmid[xx] = (pairs[z * 4 + xx, :, 256:].astype(F32) + vland[xx].astype(F32)).astype(BF)
    begin(value_last)
    wait_recv(key_copies)
    for zz in range(2):
        total = pairs[zz * 4 + x, :, :256].astype(F32)
        for d in range(3):
            total = total + kland[d * 2 + zz].astype(F32)
        kmid[zz] = total.astype(BF)
    key_last.start()
    merge_half(sq, b_t, core, dqraw, 256)
    merge_half(so, a_t, core, ob_ref, 256)
    up.middle()
    wait_recv(value_last)
    dv = vmid[x].astype(F32)
    for d in range(3):
        dv = dv + vlast[d].astype(F32)
    dvraw = dv.astype(BF)
    key_last.wait_recv()
    dkraw = turn_back(kmid[z].astype(F32) + klast[...].astype(F32))

    def columns(n, carry):
        rows = pl.ds(pl.multiple_of(n * 256, 256), 256)
        product = nt(dqraw, wq[rows, :]) + nt(dkraw, wk[rows, :]) + nt(dvraw, wv[rows, :])
        part1[:, :, rows] = product.astype(BF).reshape(8, 32, 256)
        return carry

    lax.fori_loop(0, 8, columns, 0)
    begin(scatter1())
    send_half(sk, b_t, 1 - core, dkraw, 256)
    send_half(sv, b_t, 1 - core, dvraw, 256)
    so.middle()
    sq.middle()
    merge_half(sk, b_t, core, dkraw, 256)
    merge_half(sv, b_t, core, dvraw, 256)
    fgate[...] = gate.finish()
    wait_recv(scatter1())
    result, eight = through_norm(
        x_own[...].astype(F32), dh[...], part1[t], land1, gain1_ref[...]
    )
    hidden_ref[t] = result.astype(BF)
    begin(gather_hidden())
    gain_start(eight, gbuf1, gain1_scatter)
    fdown[...] = down.finish()
    sk.middle()
    sv.middle()
    gain_middle(gbuf1, gland1, gall1, gain1_scatter, gain1_gather)
    fup[...] = up.finish()
    fo[...] = so.finish()
    fq[...] = sq.finish()
    fk[...] = sk.finish()
    fv[...] = sv.finish()
    gain_end(gall, gain2_gather, gmix_ref)
    gain_end(gall1, gain1_gather, gattn_ref)
    wait_recv(gather_block())
    wait_recv(gather_hidden())

    for copies in (scatter2, scatterm, scatter1, gather_da, gather_block, gather_hidden):
        wait_send(copies())
    for copies in (gain2_scatter, gain2_gather, gain1_scatter, gain1_gather):
        wait_send(copies())
    wait_send([pair_copy(j) for j in range(8)] + key_copies + value_copies)
    wait_send([key_last] + value_last)
    wait_send(gate.second() + gate.third())
    for one in (down, up, so, sq, sk, sv):
        one.close()


def back(*operands):
    dma = pltpu.SemaphoreType.DMA
    tokens = (8, 32, 2048)
    outs = [jax.ShapeDtypeStruct(tokens, BF)] * 2 + [jax.ShapeDtypeStruct((1, 128), F32)] * 2
    outs += [jax.ShapeDtypeStruct((256, 512), F32)] * 3
    outs += [jax.ShapeDtypeStruct((128, 256), F32)] * 4
    vmem = pltpu.VMEM
    scratch = [vmem((CTX, 256, 512), BF)] + [vmem((2048, 256), BF)] * 3 + [vmem((256, 2048), BF)]
    scratch += [vmem((32, 2048), BF)] * 3 + [vmem((32, 2048), F32)]
    scratch += [vmem((7, 32, 2048), BF)] * 3 + [vmem(tokens, BF)] * 2
    scratch += [vmem((CTX, 8, 128), F32), vmem((CTX - 1, 8, 128), F32), vmem((TP, 8, 128), F32)] * 2
    scratch += [vmem((2, 1024, 256), BF)] * 2 + [vmem((1024, 256), BF)] * 2 + [vmem((256, 256), F32)]
    for order in ("x", "z", "z"):
        scratch += spread_scratch(order, 256, 512)
    for order in SMALL:
        scratch += spread_scratch(order, 128, 256)
    scratch += [vmem((8, 256, 512), BF)]
    scratch += [vmem((6, 256, 256), BF), vmem((2, 256, 256), BF), vmem((256, 256), BF)]
    scratch += [vmem((4, 256, 256), BF), vmem((4, 256, 256), BF), vmem((3, 256, 256), BF)]
    scratch += [dma((N_SEMS,))]
    in_specs = [SMEM_SPEC] + [ANY_SPEC] * 2 + [VMEM_SPEC] * 16 + [ANY_SPEC] * 6
    return pl.pallas_call(
        back_kernel,
        out_shape=outs,
        in_specs=in_specs,
        out_specs=[VMEM_SPEC] * len(outs),
        scratch_shapes=scratch,
        compiler_params=pltpu.CompilerParams(
            collective_id=2, has_side_effects=True, vmem_limit_bytes=GRANT
        ),
        name="back",
    )(*operands)


def finish_kernel(*refs):
    ins, outs = refs[:11], refs[11:]
    block, hidden, mix, attn, gate, down, up, o, q, k, v = ins
    oblock, ohidden, oattn, oq, ok, ov, oo, omix, ogate, oup, odown = outs
    for source, target in (
        (block, oblock), (hidden, ohidden), (attn, oattn), (mix, omix), (q, oq), (k, ok), (v, ov),
    ):
        target[...] = source[...]
    oo[...] = o[...].T
    for n in range(2):
        rows, cols = slice(n * 128, (n + 1) * 128), slice(n * 512, (n + 1) * 512)
        ogate[:, cols] = gate[rows, :]
        oup[:, cols] = up[rows, :]
        odown[cols, :] = down[rows, :].T


def finish(*operands):
    f32 = lambda *s: jax.ShapeDtypeStruct(s, F32)
    tokens = jax.ShapeDtypeStruct((256, 2048), BF)
    outs = [tokens, tokens, f32(1, 128), f32(128, 256), f32(128, 256), f32(128, 256), f32(256, 128)]
    outs += [f32(1, 128), f32(128, 1024), f32(128, 1024), f32(1024, 128)]
    return pl.pallas_call(
        finish_kernel,
        out_shape=outs,
        in_specs=[VMEM_SPEC] * 11,
        out_specs=[VMEM_SPEC] * 11,
        compiler_params=pltpu.CompilerParams(vmem_limit_bytes=GRANT),
        name="finish",
    )(*operands)


def rope_tables(places):
    half_dim = HD // 2
    frequency = THETA ** (-(jnp.arange(half_dim, dtype=F32) * 2.0 / HD))
    angles = places.astype(F32)[:, None] * frequency[None, :]
    cosine, sine = jnp.cos(angles), jnp.sin(angles)
    return (
        jnp.tile(jnp.concatenate([cosine, cosine], axis=1), (1, 4)),
        jnp.tile(jnp.concatenate([-sine, sine], axis=1), (1, 4)),
    )


def shards(
    hidden_in,
    positions,
    attend_gain,
    w_query,
    w_key,
    w_value,
    w_output,
    mixing_gain,
    w_gate,
    w_up,
    w_down,
    out_cotangent,
):
    ctx_rank = lax.axis_index("ctx")
    own_places = lax.dynamic_slice_in_dim(positions, ctx_rank * 256, 256)
    cosine, sine = rope_tables(own_places)
    base = positions.reshape(32, 128)[:, 0]
    qpos = jnp.tile(own_places, 4)[None, :]
    gain_one, gain_two = attend_gain[None, :], mixing_gain[None, :]
    tokens = lambda a: a.reshape(8, 32, 2048)

    n1, q, kv_own = project(hidden_in, gain_one, w_query, w_key, w_value, cosine, sine)
    kv = gather(kv_own)
    o, lse = attend(base, q, kv, qpos)
    ob = o.astype(BF)
    n2, h = middle(ob, w_output, tokens(hidden_in), gain_two)
    n2 = n2.reshape(256, 2048)

    gate, up = nn(n2, w_gate), nn(n2, w_up)
    sigmoid = jax.nn.sigmoid(gate)
    activated = gate * sigmoid
    inner = (activated * up).astype(BF)
    mixed = nn(inner, w_down).astype(BF)
    dz = nt(out_cotangent, w_down)
    dgate = (dz * up * sigmoid * (1.0 + gate * (1.0 - sigmoid))).astype(BF)
    dup = (dz * activated).astype(BF)
    dn2 = (nt(dgate, w_gate) + nt(dup, w_up)).astype(BF)
    block_out, grad_hidden, grad_mixing, grad_attend, *grads = back(
        base, tokens(dn2), tokens(mixed), h, out_cotangent, gain_two, n2, dgate, dup, inner,
        q, qpos, lse, o, ob, w_output, cosine, sine, gain_one,
        kv, w_query, w_key, w_value, n1, hidden_in,
    )
    results = finish(
        block_out.reshape(256, 2048), grad_hidden.reshape(256, 2048), grad_mixing, grad_attend, *grads
    )
    return tuple(r.reshape(128) if r.shape == (1, 128) else r for r in results)


def solution(mesh):
    placed = (
        P("ctx", None),
        P(),
        P(),
        P(None, "tp"),
        P(None, "tp"),
        P(None, "tp"),
        P("tp", None),
        P(),
        P(None, "tp"),
        P(None, "tp"),
        P("tp", None),
        P("ctx", None),
    )
    return jax.shard_map(
        shards,
        mesh=mesh,
        in_specs=placed,
        out_specs=(
            P("ctx", None),
            P("ctx", None),
            P("ctx"),
            P("ctx", "tp"),
            P("ctx", "tp"),
            P("ctx", "tp"),
            P("tp", "ctx"),
            P("ctx"),
            P("ctx", "tp"),
            P("ctx", "tp"),
            P("tp", "ctx"),
        ),
        check_vma=False,
    )
```
